32 devices in a mesh: gx: 8 (over z, x), gy: 4 (over y, core).
Axes of the slice: x: 2, y: 2, z: 4, core: 2. Of those that a mesh axis runs over, the one named last changes fastest.
Arguments:
- field: bfloat16 [768, 128, 1536], P(None, 'gy', 'gx'), may hold values from -8 to 8
- norm_field: float32 [768, 128, 1536], P(('gx', 'gy')), may hold values from 0.5 to 2
- vertical: float32 [2, 64, 64], replicated, may hold values from -0.75 to 0.75
- x_filter: bfloat16 [1536, 1536], replicated, may hold values from -2 to 2
- y_filter: bfloat16 [768, 768], replicated, may hold values from -2 to 2
Outputs:
- covaried: bfloat16 [768, 128, 1536], P(None, 'gy', 'gx')
The draws below stay inside these ranges and needn't reach their ends.
All inputs are finite; a program needn't handle non-finite values.
Results may differ from the reference program's by a relative error of at most 0.0075.
Values may be sent and summed in bfloat16 or wider, within the bound.
A program may use at most 128 MiB of HBM per device.

```python
import math
import jax
import jax.numpy as jnp
from jax import lax

NX = 1536
NY = 768
LEVELS = 64
SPECIES = 2
COMPONENTS = 128


def draw_field(key, part):
    key = jax.random.fold_in(key, 11)
    first_key = jax.random.fold_in(key, 0)
    base = jax.random.normal(first_key, (NY, SPECIES * LEVELS, NX), jnp.float32)
    values = jnp.clip(base, -6.0, 6.0)
    return values.astype(jnp.bfloat16)


def draw_x_filter(key, part):
    key = jax.random.fold_in(key, 23)
    spots = jnp.arange(NX, dtype=jnp.float32)
    reach = NX / 4.0
    envelope = jnp.exp(-jnp.abs(spots[:, None] - spots[None, :]) / reach)
    rough = jnp.clip(jax.random.normal(key, (NX, NX), jnp.float32), -3.0, 3.0)
    return (envelope * rough / math.sqrt(reach)).astype(jnp.bfloat16)


def draw_y_filter(key, part):
    key = jax.random.fold_in(key, 29)
    spots = jnp.arange(NY, dtype=jnp.float32)
    reach = NY / 4.0
    envelope = jnp.exp(-jnp.abs(spots[:, None] - spots[None, :]) / reach)
    rough = jnp.clip(jax.random.normal(key, (NY, NY), jnp.float32), -3.0, 3.0)
    return (envelope * rough / math.sqrt(reach)).astype(jnp.bfloat16)


def shard_levels(key, extent, shards, smallest, high):
    level = 1.0
    for dim, shards_of in shards:
        steps = jax.random.uniform(jax.random.fold_in(jax.random.fold_in(key, 6), dim), (shards_of,), jnp.float32, smallest / len(shards), high / len(shards))
        level = level * jnp.repeat(jnp.exp(steps), extent[dim] // shards_of).reshape((-1,) + (1,) * (len(extent) - 1 - dim))
    return level


def scatter_about(key, shape, spread, most, kind=jnp.bfloat16):
    values = spread * jax.random.normal(key, shape, jnp.float32)
    return jnp.clip(values, min=-most, max=most).astype(kind)


def setup_inputs(seed: int = 0) -> dict:
    splits = jax.random.split(jax.random.key(seed), 6)
    return {
        "field": draw_field(jax.random.fold_in(splits[5], 71), 0),
        "norm_field": jnp.clip(jnp.exp(math.log(2.0) - 1.3862944 * jax.random.uniform(splits[1], (NY, COMPONENTS, NX), jnp.float32) ** shard_levels(splits[1], (NY, COMPONENTS, NX), ((0, 32),), -0.2, 0.2)), 0.5, 2.0),
        "vertical": scatter_about(splits[2], (SPECIES, LEVELS, LEVELS), LEVELS ** -0.5, 0.75, jnp.float32),
        "x_filter": draw_x_filter(jax.random.fold_in(splits[5], 71), 0),
        "y_filter": draw_y_filter(jax.random.fold_in(splits[5], 71), 0),
    }


def reference(field, norm_field, vertical, x_filter, y_filter):
    def one_species(index):
        start = (index * LEVELS).astype(jnp.int32)
        block = lax.dynamic_slice_in_dim(field, start, LEVELS, 1)
        scales = lax.dynamic_slice_in_dim(norm_field, start, LEVELS, 1)
        factor = vertical[index]
        first = jnp.dot(y_filter.T, block.reshape(NY, -1), preferred_element_type=jnp.float32)
        first = first.astype(jnp.bfloat16).reshape(NY, LEVELS, NX)
        second = jnp.dot(first.reshape(-1, NX), x_filter, preferred_element_type=jnp.float32)
        second = second.astype(jnp.bfloat16).reshape(NY, LEVELS, NX)
        scaled = scales * second.astype(jnp.float32)
        lowered = jnp.einsum("lk,ylx->ykx", factor, scaled, precision=lax.Precision.HIGHEST)
        raised = jnp.einsum("kl,ylx->ykx", factor, lowered, precision=lax.Precision.HIGHEST)
        middle = (scales * raised).astype(jnp.bfloat16)
        third = jnp.dot(middle.reshape(-1, NX), x_filter.T, preferred_element_type=jnp.float32)
        third = third.astype(jnp.bfloat16).reshape(NY, -1)
        result = jnp.dot(y_filter, third, preferred_element_type=jnp.float32)
        return result.astype(jnp.bfloat16).reshape(NY, LEVELS, NX)

    stacked = lax.map(one_species, jnp.arange(SPECIES, dtype=jnp.int32))
    return jnp.transpose(stacked, (1, 0, 2, 3)).reshape(NY, SPECIES * LEVELS, NX)
```

```python
import functools

import jax
import jax.numpy as jnp
from jax import lax
from jax.experimental import pallas as pl
from jax.experimental.pallas import tpu as pltpu
from jax.sharding import PartitionSpec as P

MESH = pl.DeviceIdType.MESH
LANES = 128
HALF = 64
CHUNK_ROWS = 8
TILE = 256


def xlines_forward(block, x_filter):
    width = x_filter.shape[0]
    result = jnp.dot(block.reshape(-1, width), x_filter, preferred_element_type=jnp.float32)
    return result.astype(jnp.bfloat16).reshape(block.shape)


def xlines_adjoint(block, x_filter):
    width = x_filter.shape[0]
    result = lax.dot_general(
        block.reshape(-1, width),
        x_filter,
        (((1,), (1,)), ((), ())),
        preferred_element_type=jnp.float32,
    )
    return result.astype(jnp.bfloat16).reshape(block.shape)


def columns_work(block, scales, vertical):
    species = vertical.shape[0]
    levels = vertical.shape[1]
    rows, comps, width = block.shape
    scaled = (scales * block.astype(jnp.float32)).reshape(rows, species, levels, width)
    lowered = jnp.einsum("slk,rslx->rskx", vertical, scaled, precision=lax.Precision.HIGHEST)
    raised = jnp.einsum("skl,rslx->rskx", vertical, lowered, precision=lax.Precision.HIGHEST)
    return (scales * raised.reshape(rows, comps, width)).astype(jnp.bfloat16)


def general_plan(field, norm_field, vertical, x_filter, y_filter):
    lines, comps, width = field.shape
    first = lax.dot_general(
        y_filter,
        field.reshape(lines, comps * width),
        (((0,), (0,)), ((), ())),
        preferred_element_type=jnp.float32,
    )
    first = first.astype(jnp.bfloat16).reshape(lines, comps, width)
    xblock = lax.all_to_all(first, "gx", split_axis=0, concat_axis=2, tiled=True)
    second = xlines_forward(xblock, x_filter)
    columns = lax.all_to_all(second, "gy", split_axis=0, concat_axis=1, tiled=True)
    middle = columns_work(columns, norm_field, vertical)
    returned = lax.all_to_all(middle, "gy", split_axis=1, concat_axis=0, tiled=True)
    third = xlines_adjoint(returned, x_filter)
    ylines = lax.all_to_all(third, "gx", split_axis=2, concat_axis=0, tiled=True)
    result = jnp.dot(
        y_filter, ylines.reshape(lines, comps * width), preferred_element_type=jnp.float32
    )
    return result.astype(jnp.bfloat16).reshape(lines, comps, width)


def exchange_kernel(
    gx, gy, first, norm, xf, factor, ylines,
    xb, sec, col, ret, xs, nbuf,
    b_send, b_recv, d_send, d_recv, e_send, e_recv, f_send, f_recv, own, nsem,
):
    chunks, _, rows, _, comps_half, _ = xb.shape
    comps = 2 * comps_half
    width = xf.shape[1]
    species, levels, _ = factor.shape
    me_x = lax.axis_index("gx")
    me_y = lax.axis_index("gy")
    whole_a = gx * LANES
    part_b = gx * HALF
    m = rows * comps_half

    barrier = pltpu.get_barrier_semaphore()
    for s in range(1, gx):
        pl.semaphore_signal(
            barrier, inc=1, device_id={"gx": lax.rem(me_x + s, gx)}, device_id_type=MESH)
    for s in range(1, gy):
        pl.semaphore_signal(
            barrier, inc=1, device_id={"gy": lax.rem(me_y + s, gy)}, device_id_type=MESH)
    pl.semaphore_wait(barrier, gx + gy - 2)

    def remote(src, dst, send, recv, axis, peer):
        return pltpu.make_async_remote_copy(
            src_ref=src, dst_ref=dst, send_sem=send, recv_sem=recv,
            device_id={axis: peer}, device_id_type=MESH)

    def out_x(j):
        copies = []
        for s in range(1, gx):
            peer = lax.rem(me_x + s, gx)
            copies.append(remote(first.at[j, peer], xb.at[j, me_x],
                                 b_send.at[j, s - 1], b_recv.at[j, s - 1], "gx", peer))
        mine = pltpu.make_async_copy(first.at[j, me_x], xb.at[j, me_x], own.at[0, j])
        return copies, mine

    def out_y(j):
        copies = []
        for s in range(1, gy):
            peer = lax.rem(me_y + s, gy)
            copies.append(remote(
                sec.at[j, pl.ds(peer * CHUNK_ROWS, CHUNK_ROWS)],
                col.at[j, :, pl.ds(pl.multiple_of(me_y * comps, comps), comps), :],
                d_send.at[j, s - 1], d_recv.at[j, s - 1], "gy", peer))
        mine = pltpu.make_async_copy(
            sec.at[j, pl.ds(me_y * CHUNK_ROWS, CHUNK_ROWS)],
            col.at[j, :, pl.ds(pl.multiple_of(me_y * comps, comps), comps), :], own.at[1, j])
        return copies, mine

    def back_y(j):
        copies = []
        for s in range(1, gy):
            peer = lax.rem(me_y + s, gy)
            copies.append(remote(
                col.at[j, :, pl.ds(pl.multiple_of(peer * comps, comps), comps), :],
                ret.at[j, pl.ds(me_y * CHUNK_ROWS, CHUNK_ROWS)],
                e_send.at[j, s - 1], e_recv.at[j, s - 1], "gy", peer))
        mine = pltpu.make_async_copy(
            col.at[j, :, pl.ds(pl.multiple_of(me_y * comps, comps), comps), :],
            ret.at[j, pl.ds(me_y * CHUNK_ROWS, CHUNK_ROWS)], own.at[2, j])
        return copies, mine

    def back_x(j):
        copies = []
        for s in range(1, gx):
            peer = lax.rem(me_x + s, gx)
            copies.append(remote(xb.at[j, peer], ylines.at[j, me_x],
                                 f_send.at[j, s - 1], f_recv.at[j, s - 1], "gx", peer))
        mine = pltpu.make_async_copy(xb.at[j, me_x], ylines.at[j, me_x], own.at[3, j])
        return copies, mine

    def start(pair):
        for copy in pair[0]:
            copy.start()
        pair[1].start()
        return pair

    def arrive(pair):
        for copy in pair[0]:
            copy.wait_recv()
        pair[1].wait()

    def drain(pair):
        for copy in pair[0]:
            copy.wait_send()

    def norm_load(j):
        return pltpu.make_async_copy(norm.at[pl.ds(j * CHUNK_ROWS, CHUNK_ROWS)], nbuf, nsem)

    def low_lanes(shape):
        return lax.broadcasted_iota(jnp.int32, shape, len(shape) - 1) < HALF

    def forward(j):
        for h in range(2):
            for g in range(gx):
                xs[:, g * LANES:(g + 1) * LANES] = xb[j, g, :, h].reshape(m, LANES)
            for q in range(gx // 2):
                even = xb[j, 2 * q, :, 2].reshape(m, LANES)
                odd = xb[j, 2 * q + 1, :, 2].reshape(m, LANES)
                low, high = (even, odd) if h == 0 else (odd, even)
                at = whole_a + q * LANES
                xs[:, at:at + LANES] = jnp.where(low_lanes((m, LANES)), low, high)
            base = whole_a + part_b * h

            @pl.loop(0, width // TILE)
            def _(n):
                cols = pl.ds(pl.multiple_of(n * TILE, TILE), TILE)
                acc = jnp.dot(xs[:, :whole_a], xf[:whole_a, cols],
                              preferred_element_type=jnp.float32)
                acc += jnp.dot(xs[:, whole_a:], xf[base:base + part_b, cols],
                               preferred_element_type=jnp.float32)
                sec[j, :, h * comps_half:(h + 1) * comps_half, cols] = (
                    acc.astype(jnp.bfloat16).reshape(rows, comps_half, TILE))

    def columns(j):
        @pl.loop(0, CHUNK_ROWS)
        def _(r):
            for s in range(species):
                here = slice(s * levels, (s + 1) * levels)
                for n in range(0, width, 2 * TILE):
                    lanes = slice(n, n + 2 * TILE)
                    scales = nbuf[r, here, lanes]
                    scaled = scales * col[j, r, here, lanes].astype(jnp.float32)
                    high = scaled.astype(jnp.bfloat16)
                    low = (scaled - high.astype(jnp.float32)).astype(jnp.bfloat16)
                    stack = jnp.concatenate([high, high, low], axis=0)
                    raised = jnp.dot(factor[s], stack, preferred_element_type=jnp.float32)
                    col[j, r, here, lanes] = (scales * raised).astype(jnp.bfloat16)

    def adjoint(j):
        def lines(h):
            return ret[j, :, h * comps_half:(h + 1) * comps_half, :].reshape(m, width)

        def dots(block, at):
            return lax.dot_general(block, xf[pl.ds(at, TILE), :], (((1,), (1,)), ((), ())),
                                   preferred_element_type=jnp.float32)

        for h in range(2):
            @pl.loop(0, whole_a // TILE)
            def _(n):
                part = dots(lines(h), pl.multiple_of(n * TILE, TILE))
                for i in range(TILE // LANES):
                    xb[j, n * (TILE // LANES) + i, :, h] = (
                        part[:, i * LANES:(i + 1) * LANES].astype(jnp.bfloat16)
                        .reshape(rows, comps_half, LANES))

        @pl.loop(0, part_b // TILE)
        def _(n):
            at = pl.multiple_of(whole_a + n * TILE, TILE)
            part0 = dots(lines(0), at)
            part1 = dots(lines(1), pl.multiple_of(at + part_b, TILE))
            for i in range(TILE // LANES):
                p0 = part0[:, i * LANES:(i + 1) * LANES]
                p1 = part1[:, i * LANES:(i + 1) * LANES]
                mask = low_lanes((m, LANES))
                g = 2 * (n * (TILE // LANES) + i)
                xb[j, g, :, 2] = jnp.where(mask, p0, p1).astype(jnp.bfloat16).reshape(
                    rows, comps_half, LANES)
                xb[j, g + 1, :, 2] = jnp.where(mask, p1, p0).astype(jnp.bfloat16).reshape(
                    rows, comps_half, LANES)

    bs, ds, es, fs = {}, {}, {}, {}

    def stage_c(j):
        arrive(bs[j])
        if j + 2 < chunks:
            bs[j + 2] = start(out_x(j + 2))
        forward(j)
        ds[j] = start(out_y(j))

    def stage_e(j):
        arrive(ds[j])
        norm_load(j).wait()
        columns(j)
        es[j] = start(back_y(j))
        if j + 1 < chunks:
            norm_load(j + 1).start()

    def stage_f(j):
        arrive(es[j])
        adjoint(j)
        fs[j] = start(back_x(j))

    norm_load(0).start()
    for j in range(min(2, chunks)):
        bs[j] = start(out_x(j))
    stage_c(0)
    stage_e(0)
    for j in range(1, chunks):
        stage_c(j)
        stage_f(j - 1)
        stage_e(j)
    stage_f(chunks - 1)
    for j in range(chunks):
        arrive(fs[j])
    for j in range(chunks):
        for pair in (bs[j], ds[j], es[j], fs[j]):
            drain(pair)


def exchange(gx, gy, first, norm_field, xf, factor):
    chunks, _, rows, _, comps_half, _ = first.shape
    width = xf.shape[1]
    dma = pltpu.SemaphoreType.DMA
    all_comps = norm_field.shape[1]
    return pl.pallas_call(
        functools.partial(exchange_kernel, gx, gy),
        out_shape=jax.ShapeDtypeStruct(first.shape, jnp.bfloat16),
        in_specs=[
            pl.BlockSpec(memory_space=pl.ANY),
            pl.BlockSpec(memory_space=pl.ANY),
            pl.BlockSpec(memory_space=pltpu.VMEM),
            pl.BlockSpec(memory_space=pltpu.VMEM),
        ],
        out_specs=pl.BlockSpec(memory_space=pl.ANY),
        scratch_shapes=[
            pltpu.VMEM(first.shape, jnp.bfloat16),
            pltpu.VMEM((chunks, rows, 2 * comps_half, width), jnp.bfloat16),
            pltpu.VMEM((chunks, CHUNK_ROWS, all_comps, width), jnp.bfloat16),
            pltpu.VMEM((chunks, rows, 2 * comps_half, width), jnp.bfloat16),
            pltpu.VMEM((rows * comps_half, width), jnp.bfloat16),
            pltpu.VMEM((CHUNK_ROWS, all_comps, width), jnp.float32),
            dma((chunks, gx - 1)), dma((chunks, gx - 1)),
            dma((chunks, gy - 1)), dma((chunks, gy - 1)),
            dma((chunks, gy - 1)), dma((chunks, gy - 1)),
            dma((chunks, gx - 1)), dma((chunks, gx - 1)),
            dma((4, chunks)), dma,
        ],
        compiler_params=pltpu.CompilerParams(
            collective_id=0, has_side_effects=True, vmem_limit_bytes=60 * 1024 * 1024),
        name="exchange",
    )(first, norm_field, xf, factor)


def pack(block, odd):
    half = block.shape[1] // 2
    b0, b1 = block[:, :half, LANES:], block[:, half:, LANES:]
    tail = jnp.where(odd, jnp.concatenate([b1, b0], 2), jnp.concatenate([b0, b1], 2))
    return jnp.concatenate([block[:, :half, :LANES], block[:, half:, :LANES], tail], 1)


def unpack(block, odd):
    half = block.shape[1] // 3
    tail = block[:, 2 * half:]
    low, high = tail[:, :, :HALF], tail[:, :, HALF:]
    b0, b1 = jnp.where(odd, high, low), jnp.where(odd, low, high)
    return jnp.concatenate([
        jnp.concatenate([block[:, :half], b0], 2),
        jnp.concatenate([block[:, half:2 * half], b1], 2)], 1)


def fused_plan(gx, gy, field, norm_field, vertical, x_filter, y_filter):
    lines, comps, width = field.shape
    chunks = norm_field.shape[0] // CHUNK_ROWS
    half = comps // 2
    odd = lax.rem(lax.axis_index("gx"), 2) == 1

    product = jnp.einsum("skl,sml->skm", vertical, vertical, precision=lax.Precision.HIGHEST)
    high = lax.reduce_precision(product, 8, 7)
    low = product - high
    factor = jnp.concatenate([high, low, high], 2).astype(jnp.bfloat16)

    strips = x_filter.reshape(gx, width, -1)
    tails = strips[:, LANES:].reshape(gx // 2, 2, HALF, -1)
    xf = jnp.concatenate([
        strips[:, :LANES].reshape(gx * LANES, -1),
        tails.reshape(gx * HALF, -1),
        tails[:, ::-1].reshape(gx * HALF, -1)], 0)

    yf = y_filter.reshape(lines, gx, gy, chunks, CHUNK_ROWS)
    yf = yf.transpose(0, 3, 1, 2, 4).reshape(lines, lines)

    packed = pack(field, odd)
    first = lax.dot_general(
        yf, packed, (((0,), (0,)), ((), ())), preferred_element_type=jnp.float32)
    first = first.astype(jnp.bfloat16).reshape(
        chunks, gx, gy * CHUNK_ROWS, 3, half, LANES)
    ylines = exchange(gx, gy, first, norm_field, xf, factor)
    ylines = ylines.reshape(lines, 3 * half, LANES)
    result = lax.dot_general(
        yf, ylines, (((1,), (0,)), ((), ())), preferred_element_type=jnp.float32)
    return unpack(result.astype(jnp.bfloat16), odd)


def per_device(gx, gy, field, norm_field, vertical, x_filter, y_filter):
    lines, comps, width = field.shape
    rows, all_comps, whole = norm_field.shape
    fits = (
        width == LANES + HALF and comps == 32 and rows % CHUNK_ROWS == 0 and gx % 4 == 0
        and gy > 1 and whole % (2 * TILE) == 0 and vertical.shape[1] % 16 == 0
        and rows * all_comps * whole <= 24 * 128 * 1536
    )
    if fits:
        return fused_plan(gx, gy, field, norm_field, vertical, x_filter, y_filter)
    return general_plan(field, norm_field, vertical, x_filter, y_filter)


def solution(mesh):
    return jax.shard_map(
        functools.partial(per_device, mesh.shape["gx"], mesh.shape["gy"]),
        mesh=mesh,
        in_specs=(P(None, "gy", "gx"), P(("gx", "gy"), None, None), P(), P(), P()),
        out_specs=P(None, "gy", "gx"),
        check_vma=False,
    )
```

```python
import functools

import jax
import jax.numpy as jnp
from jax import lax
from jax.experimental import pallas as pl
from jax.experimental.pallas import tpu as pltpu
from jax.sharding import PartitionSpec as P

MESH = pl.DeviceIdType.MESH
LANES = 128
HALF = 64
CHUNK_ROWS = 8
TILE = 256


def xlines_forward(block, x_filter):
    width = x_filter.shape[0]
    result = jnp.dot(block.reshape(-1, width), x_filter, preferred_element_type=jnp.float32)
    return result.astype(jnp.bfloat16).reshape(block.shape)


def xlines_adjoint(block, x_filter):
    width = x_filter.shape[0]
    result = lax.dot_general(
        block.reshape(-1, width),
        x_filter,
        (((1,), (1,)), ((), ())),
        preferred_element_type=jnp.float32,
    )
    return result.astype(jnp.bfloat16).reshape(block.shape)


def columns_work(block, scales, vertical):
    species = vertical.shape[0]
    levels = vertical.shape[1]
    rows, comps, width = block.shape
    scaled = (scales * block.astype(jnp.float32)).reshape(rows, species, levels, width)
    lowered = jnp.einsum("slk,rslx->rskx", vertical, scaled, precision=lax.Precision.HIGHEST)
    raised = jnp.einsum("skl,rslx->rskx", vertical, lowered, precision=lax.Precision.HIGHEST)
    return (scales * raised.reshape(rows, comps, width)).astype(jnp.bfloat16)


def general_plan(field, norm_field, vertical, x_filter, y_filter):
    lines, comps, width = field.shape
    first = lax.dot_general(
        y_filter,
        field.reshape(lines, comps * width),
        (((0,), (0,)), ((), ())),
        preferred_element_type=jnp.float32,
    )
    first = first.astype(jnp.bfloat16).reshape(lines, comps, width)
    xblock = lax.all_to_all(first, "gx", split_axis=0, concat_axis=2, tiled=True)
    second = xlines_forward(xblock, x_filter)
    columns = lax.all_to_all(second, "gy", split_axis=0, concat_axis=1, tiled=True)
    middle = columns_work(columns, norm_field, vertical)
    returned = lax.all_to_all(middle, "gy", split_axis=1, concat_axis=0, tiled=True)
    third = xlines_adjoint(returned, x_filter)
    ylines = lax.all_to_all(third, "gx", split_axis=2, concat_axis=0, tiled=True)
    result = jnp.dot(
        y_filter, ylines.reshape(lines, comps * width), preferred_element_type=jnp.float32
    )
    return result.astype(jnp.bfloat16).reshape(lines, comps, width)


def exchange_kernel(
    gx, gy, first, norm, x_filter, factor, ylines,
    xb, sec, col, ret, xs, nbuf, xf, spread,
    b_send, b_recv, d_send, d_recv, e_send, e_recv, f_send, f_recv, own, nsem, xsem,
):
    chunks, _, _, comps_half, rows, _ = xb.shape
    comps = 2 * comps_half
    width = xf.shape[1]
    species, levels, _ = factor.shape
    me_x = lax.axis_index("gx")
    me_y = lax.axis_index("gy")
    whole_a = gx * LANES
    part_b = gx * HALF
    m = rows * comps_half

    strip = LANES + HALF
    xf_copies = []
    for g in range(gx):
        tail = x_filter.at[pl.ds(g * strip + LANES, HALF)]
        for src, at in (
            (x_filter.at[pl.ds(g * strip, LANES)], g * LANES),
            (tail, whole_a + g * HALF),
            (tail, whole_a + part_b + (g ^ 1) * HALF),
        ):
            xf_copies.append(pltpu.make_async_copy(
                src, xf.at[pl.ds(at, src.shape[0])], xsem.at[len(xf_copies)]))

    barrier = pltpu.get_barrier_semaphore()
    for s in range(1, gx):
        pl.semaphore_signal(
            barrier, inc=1, device_id={"gx": lax.rem(me_x + s, gx)}, device_id_type=MESH)
    for s in range(1, gy):
        pl.semaphore_signal(
            barrier, inc=1, device_id={"gy": lax.rem(me_y + s, gy)}, device_id_type=MESH)
    pl.semaphore_wait(barrier, gx + gy - 2)

    def remote(src, dst, send, recv, axis, peer):
        return pltpu.make_async_remote_copy(
            src_ref=src, dst_ref=dst, send_sem=send, recv_sem=recv,
            device_id={axis: peer}, device_id_type=MESH)

    def lines_of(ref, j, g):
        return ref.at[:, :, pl.ds(pl.multiple_of((j * gx + g) * rows, rows), rows), :]

    def out_x(j):
        copies = []
        for s in range(1, gx):
            peer = lax.rem(me_x + s, gx)
            copies.append(remote(lines_of(first, j, peer), xb.at[j, me_x],
                                 b_send.at[j, s - 1], b_recv.at[j, s - 1], "gx", peer))
        mine = pltpu.make_async_copy(lines_of(first, j, me_x), xb.at[j, me_x], own.at[0, j])
        return copies, mine

    def out_y(j):
        copies = []
        for s in range(1, gy):
            peer = lax.rem(me_y + s, gy)
            copies.append(remote(
                sec.at[j, pl.ds(peer * CHUNK_ROWS, CHUNK_ROWS)],
                col.at[j, :, pl.ds(pl.multiple_of(me_y * comps, comps), comps), :],
                d_send.at[j, s - 1], d_recv.at[j, s - 1], "gy", peer))
        mine = pltpu.make_async_copy(
            sec.at[j, pl.ds(me_y * CHUNK_ROWS, CHUNK_ROWS)],
            col.at[j, :, pl.ds(pl.multiple_of(me_y * comps, comps), comps), :], own.at[1, j])
        return copies, mine

    def back_y(j):
        copies = []
        for s in range(1, gy):
            peer = lax.rem(me_y + s, gy)
            copies.append(remote(
                col.at[j, :, pl.ds(pl.multiple_of(peer * comps, comps), comps), :],
                ret.at[j, pl.ds(me_y * CHUNK_ROWS, CHUNK_ROWS)],
                e_send.at[j, s - 1], e_recv.at[j, s - 1], "gy", peer))
        mine = pltpu.make_async_copy(
            col.at[j, :, pl.ds(pl.multiple_of(me_y * comps, comps), comps), :],
            ret.at[j, pl.ds(me_y * CHUNK_ROWS, CHUNK_ROWS)], own.at[2, j])
        return copies, mine

    def back_x(j):
        copies = []
        for s in range(1, gx):
            peer = lax.rem(me_x + s, gx)
            copies.append(remote(xb.at[j, peer], lines_of(ylines, j, me_x),
                                 f_send.at[j, s - 1], f_recv.at[j, s - 1], "gx", peer))
        mine = pltpu.make_async_copy(xb.at[j, me_x], lines_of(ylines, j, me_x), own.at[3, j])
        return copies, mine

    def start(pair):
        for copy in pair[0]:
            copy.start()
        pair[1].start()
        return pair

    def arrive(pair):
        for copy in pair[0]:
            copy.wait_recv()
        pair[1].wait()

    def drain(pair):
        for copy in pair[0]:
            copy.wait_send()

    def norm_load(j):
        return pltpu.make_async_copy(norm.at[pl.ds(j * CHUNK_ROWS, CHUNK_ROWS)], nbuf, nsem)

    def low_lanes(shape):
        return lax.broadcasted_iota(jnp.int32, shape, len(shape) - 1) < HALF

    def forward(j):
        for h in range(2):
            for g in range(gx):
                xs[:, g * LANES:(g + 1) * LANES] = xb[j, g, h].reshape(m, LANES)
            for q in range(gx // 2):
                even = xb[j, 2 * q, 2].reshape(m, LANES)
                odd = xb[j, 2 * q + 1, 2].reshape(m, LANES)
                low, high = (even, odd) if h == 0 else (odd, even)
                at = whole_a + q * LANES
                xs[:, at:at + LANES] = jnp.where(low_lanes((m, LANES)), low, high)
            base = whole_a + part_b * h

            @pl.loop(0, width // TILE)
            def _(n):
                cols = pl.ds(pl.multiple_of(n * TILE, TILE), TILE)
                acc = jnp.dot(xs[:, :whole_a], xf[:whole_a, cols],
                              preferred_element_type=jnp.float32)
                acc += jnp.dot(xs[:, whole_a:], xf[base:base + part_b, cols],
                               preferred_element_type=jnp.float32)
                for i in range(TILE // LANES):
                    spread[i] = acc[:, i * LANES:(i + 1) * LANES]
                for i in range(TILE // LANES):
                    lanes = pl.ds(pl.multiple_of(n * TILE + i * LANES, LANES), LANES)
                    for y in range(rows):
                        line = spread[i, pl.ds(y, comps_half, stride=rows), :]
                        sec[j, y, h * comps_half:(h + 1) * comps_half, lanes] = (
                            line.astype(jnp.bfloat16))

    def columns(j):
        @pl.loop(0, CHUNK_ROWS)
        def _(r):
            for s in range(species):
                here = slice(s * levels, (s + 1) * levels)
                for n in range(0, width, 2 * TILE):
                    lanes = slice(n, n + 2 * TILE)
                    scales = nbuf[r, here, lanes]
                    scaled = scales * col[j, r, here, lanes].astype(jnp.float32)
                    high = scaled.astype(jnp.bfloat16)
                    low = (scaled - high.astype(jnp.float32)).astype(jnp.bfloat16)
                    stack = jnp.concatenate([high, high, low], axis=0)
                    raised = jnp.dot(factor[s], stack, preferred_element_type=jnp.float32)
                    col[j, r, here, lanes] = (scales * raised).astype(jnp.bfloat16)

    def adjoint(j):
        def lines(h):
            return ret[j, :, h * comps_half:(h + 1) * comps_half, :].reshape(m, width)

        def put(part, g, t, i):
            spread[i] = part
            for c in range(comps_half):
                line = spread[i, pl.ds(c, rows, stride=comps_half), :]
                xb[j, g, t, c] = line.astype(jnp.bfloat16)

        def dots(block, at):
            return lax.dot_general(block, xf[pl.ds(at, TILE), :], (((1,), (1,)), ((), ())),
                                   preferred_element_type=jnp.float32)

        for h in range(2):
            @pl.loop(0, whole_a // TILE)
            def _(n):
                part = dots(lines(h), pl.multiple_of(n * TILE, TILE))
                for i in range(TILE // LANES):
                    put(part[:, i * LANES:(i + 1) * LANES], n * (TILE // LANES) + i, h, i)

        @pl.loop(0, part_b // TILE)
        def _(n):
            at = pl.multiple_of(whole_a + n * TILE, TILE)
            part0 = dots(lines(0), at)
            part1 = dots(lines(1), pl.multiple_of(at + part_b, TILE))
            for i in range(TILE // LANES):
                p0 = part0[:, i * LANES:(i + 1) * LANES]
                p1 = part1[:, i * LANES:(i + 1) * LANES]
                mask = low_lanes((m, LANES))
                g = 2 * (n * (TILE // LANES) + i)
                put(jnp.where(mask, p0, p1), g, 2, 0)
                put(jnp.where(mask, p1, p0), g + 1, 2, 1)

    bs, ds, es, fs = {}, {}, {}, {}

    def stage_c(j):
        arrive(bs[j])
        if j + 2 < chunks:
            bs[j + 2] = start(out_x(j + 2))
        forward(j)
        ds[j] = start(out_y(j))

    def stage_e(j):
        arrive(ds[j])
        norm_load(j).wait()
        columns(j)
        es[j] = start(back_y(j))
        if j + 1 < chunks:
            norm_load(j + 1).start()

    def stage_f(j):
        arrive(es[j])
        adjoint(j)
        fs[j] = start(back_x(j))

    for j in range(min(2, chunks)):
        bs[j] = start(out_x(j))
    for copy in xf_copies:
        copy.start()
    norm_load(0).start()
    for copy in xf_copies:
        copy.wait()
    stage_c(0)
    stage_e(0)
    for j in range(1, chunks):
        stage_c(j)
        stage_f(j - 1)
        stage_e(j)
    stage_f(chunks - 1)
    for j in range(chunks):
        arrive(fs[j])
    for j in range(chunks):
        for pair in (bs[j], ds[j], es[j], fs[j]):
            drain(pair)


def exchange(gx, gy, first, norm_field, x_filter, factor):
    _, comps_half, lines, _ = first.shape
    rows = gy * CHUNK_ROWS
    chunks = lines // (gx * rows)
    width = x_filter.shape[1]
    dma = pltpu.SemaphoreType.DMA
    all_comps = norm_field.shape[1]
    return pl.pallas_call(
        functools.partial(exchange_kernel, gx, gy),
        out_shape=jax.ShapeDtypeStruct(first.shape, jnp.bfloat16),
        in_specs=[
            pl.BlockSpec(memory_space=pl.ANY),
            pl.BlockSpec(memory_space=pl.ANY),
            pl.BlockSpec(memory_space=pl.ANY),
            pl.BlockSpec(memory_space=pltpu.VMEM),
        ],
        out_specs=pl.BlockSpec(memory_space=pl.ANY),
        scratch_shapes=[
            pltpu.VMEM((chunks, gx, 3, comps_half, rows, LANES), jnp.bfloat16),
            pltpu.VMEM((chunks, rows, 2 * comps_half, width), jnp.bfloat16),
            pltpu.VMEM((chunks, CHUNK_ROWS, all_comps, width), jnp.bfloat16),
            pltpu.VMEM((chunks, rows, 2 * comps_half, width), jnp.bfloat16),
            pltpu.VMEM((rows * comps_half, width), jnp.bfloat16),
            pltpu.VMEM((CHUNK_ROWS, all_comps, width), jnp.float32),
            pltpu.VMEM((gx * (LANES + 2 * HALF), width), jnp.bfloat16),
            pltpu.VMEM((TILE // LANES, rows * comps_half, LANES), jnp.float32),
            dma((chunks, gx - 1)), dma((chunks, gx - 1)),
            dma((chunks, gy - 1)), dma((chunks, gy - 1)),
            dma((chunks, gy - 1)), dma((chunks, gy - 1)),
            dma((chunks, gx - 1)), dma((chunks, gx - 1)),
            dma((4, chunks)), dma, dma((3 * gx,)),
        ],
        compiler_params=pltpu.CompilerParams(
            collective_id=0, has_side_effects=True, vmem_limit_bytes=60 * 1024 * 1024),
        name="exchange",
    )(first, norm_field, x_filter, factor)


def first_kernel(yf, field, first):
    odd = lax.rem(lax.axis_index("gx"), 2)
    comps = field.shape[1]
    parts = [field[h, c, :LANES, :] for h in range(2) for c in range(comps)]
    for c in range(comps):
        parts += [field[odd, c, LANES:, :], field[1 - odd, c, LANES:, :]]
    result = lax.dot_general(yf[...], jnp.concatenate(parts, 0), (((1,), (1,)), ((), ())),
                             preferred_element_type=jnp.float32)
    for t in range(3):
        for c in range(comps):
            at = (t * comps + c) * LANES
            first[t, c] = result[:, at:at + LANES].astype(jnp.bfloat16)


def first_lines(yf, field):
    _, half, strip, lines = field.shape
    step = 2
    return pl.pallas_call(
        first_kernel,
        grid=(half // step,),
        out_shape=jax.ShapeDtypeStruct((3, half, lines, LANES), jnp.bfloat16),
        in_specs=[
            pl.BlockSpec((lines, lines), lambda i: (0, 0)),
            pl.BlockSpec((2, step, strip, lines), lambda i: (0, i, 0, 0)),
        ],
        out_specs=pl.BlockSpec((3, step, lines, LANES), lambda i: (0, i, 0, 0)),
        compiler_params=pltpu.CompilerParams(vmem_limit_bytes=48 * 1024 * 1024),
        name="first_lines",
    )(yf, field)


def last_kernel(yf, ylines, result):
    odd = lax.rem(lax.axis_index("gx"), 2)
    comps = ylines.shape[1]
    lines = jnp.concatenate(
        [ylines[t, c] for t in range(3) for c in range(comps)], 1)
    total = jnp.dot(lines.T, yf[...], preferred_element_type=jnp.float32).astype(jnp.bfloat16)
    for c in range(comps):
        for h in range(2):
            at = (h * comps + c) * LANES
            result[h, c, :LANES, :] = total[at:at + LANES]
        at = (2 * comps + c) * LANES
        result[odd, c, LANES:, :] = total[at:at + HALF]
        result[1 - odd, c, LANES:, :] = total[at + HALF:at + LANES]


def last_lines(yf, ylines):
    _, half, lines, _ = ylines.shape
    strip = LANES + HALF
    step = 2
    return pl.pallas_call(
        last_kernel,
        grid=(half // step,),
        out_shape=jax.ShapeDtypeStruct((2, half, strip, lines), jnp.bfloat16),
        in_specs=[
            pl.BlockSpec((lines, lines), lambda i: (0, 0)),
            pl.BlockSpec((3, step, lines, LANES), lambda i: (0, i, 0, 0)),
        ],
        out_specs=pl.BlockSpec((2, step, strip, lines), lambda i: (0, i, 0, 0)),
        compiler_params=pltpu.CompilerParams(vmem_limit_bytes=48 * 1024 * 1024),
        name="last_lines",
    )(yf, ylines)


def fused_plan(gx, gy, field, norm_field, vertical, x_filter, y_filter):
    lines, comps, width = field.shape
    chunks = norm_field.shape[0] // CHUNK_ROWS
    half = comps // 2

    product = jnp.einsum("skl,sml->skm", vertical, vertical, precision=lax.Precision.HIGHEST)
    high = lax.reduce_precision(product, 8, 7)
    low = product - high
    factor = jnp.concatenate([high, low, high], 2).astype(jnp.bfloat16)

    yf = y_filter.reshape(lines, gx, gy, chunks, CHUNK_ROWS)
    yf = yf.transpose(3, 1, 2, 4, 0).reshape(lines, lines)

    first = first_lines(yf, field.transpose(1, 2, 0).reshape(2, half, width, lines))
    ylines = exchange(gx, gy, first, norm_field, x_filter, factor)
    result = last_lines(yf, ylines)
    return result.reshape(comps, width, lines).transpose(2, 0, 1)


def per_device(gx, gy, field, norm_field, vertical, x_filter, y_filter):
    lines, comps, width = field.shape
    rows, all_comps, whole = norm_field.shape
    fits = (
        width == LANES + HALF and comps == 32 and rows % CHUNK_ROWS == 0 and gx % 4 == 0
        and gy > 1 and whole % (2 * TILE) == 0 and vertical.shape[1] % 16 == 0
        and rows * all_comps * whole <= 24 * 128 * 1536
    )
    if fits:
        return fused_plan(gx, gy, field, norm_field, vertical, x_filter, y_filter)
    return general_plan(field, norm_field, vertical, x_filter, y_filter)


def solution(mesh):
    return jax.shard_map(
        functools.partial(per_device, mesh.shape["gx"], mesh.shape["gy"]),
        mesh=mesh,
        in_specs=(P(None, "gy", "gx"), P(("gx", "gy"), None, None), P(), P(), P()),
        out_specs=P(None, "gy", "gx"),
        check_vma=False,
    )
```

```python
import functools

import jax
import jax.numpy as jnp
from jax import lax
from jax.experimental import pallas as pl
from jax.experimental.pallas import tpu as pltpu
from jax.sharding import PartitionSpec as P

MESH = pl.DeviceIdType.MESH
LANES = 128
HALF = 64
CHUNK_ROWS = 4
SLOTS = 3
STEP = 2
TILE = 256


def xlines_forward(block, x_filter):
    width = x_filter.shape[0]
    result = jnp.dot(block.reshape(-1, width), x_filter, preferred_element_type=jnp.float32)
    return result.astype(jnp.bfloat16).reshape(block.shape)


def xlines_adjoint(block, x_filter):
    width = x_filter.shape[0]
    result = lax.dot_general(
        block.reshape(-1, width),
        x_filter,
        (((1,), (1,)), ((), ())),
        preferred_element_type=jnp.float32,
    )
    return result.astype(jnp.bfloat16).reshape(block.shape)


def columns_work(block, scales, vertical):
    species = vertical.shape[0]
    levels = vertical.shape[1]
    rows, comps, width = block.shape
    scaled = (scales * block.astype(jnp.float32)).reshape(rows, species, levels, width)
    lowered = jnp.einsum("slk,rslx->rskx", vertical, scaled, precision=lax.Precision.HIGHEST)
    raised = jnp.einsum("skl,rslx->rskx", vertical, lowered, precision=lax.Precision.HIGHEST)
    return (scales * raised.reshape(rows, comps, width)).astype(jnp.bfloat16)


def general_plan(field, norm_field, vertical, x_filter, y_filter):
    lines, comps, width = field.shape
    first = lax.dot_general(
        y_filter,
        field.reshape(lines, comps * width),
        (((0,), (0,)), ((), ())),
        preferred_element_type=jnp.float32,
    )
    first = first.astype(jnp.bfloat16).reshape(lines, comps, width)
    xblock = lax.all_to_all(first, "gx", split_axis=0, concat_axis=2, tiled=True)
    second = xlines_forward(xblock, x_filter)
    columns = lax.all_to_all(second, "gy", split_axis=0, concat_axis=1, tiled=True)
    middle = columns_work(columns, norm_field, vertical)
    returned = lax.all_to_all(middle, "gy", split_axis=1, concat_axis=0, tiled=True)
    third = xlines_adjoint(returned, x_filter)
    ylines = lax.all_to_all(third, "gx", split_axis=2, concat_axis=0, tiled=True)
    result = jnp.dot(
        y_filter, ylines.reshape(lines, comps * width), preferred_element_type=jnp.float32
    )
    return result.astype(jnp.bfloat16).reshape(lines, comps, width)


def exchange_kernel(
    gx, gy, field_in, norm, x_filter, factor, yf, ylines,
    xb, sec, col, ret, xs, nbuf, xf, spread, field, first,
    b_send, b_recv, d_send, d_recv, e_send, e_recv, f_send, f_recv, own, nsem, xsem, fsem,
):
    chunks, _, _, comps_half, rows, _ = xb.shape
    comps = 2 * comps_half
    width = xf.shape[1]
    species, levels, _ = factor.shape
    me_x = lax.axis_index("gx")
    me_y = lax.axis_index("gy")
    whole_a = gx * LANES
    part_b = gx * HALF
    m = rows * comps_half

    strip = LANES + HALF
    xf_copies = []
    for g in range(gx):
        tail = x_filter.at[pl.ds(g * strip + LANES, HALF)]
        for src, at in (
            (x_filter.at[pl.ds(g * strip, LANES)], g * LANES),
            (tail, whole_a + g * HALF),
            (tail, whole_a + part_b + (g ^ 1) * HALF),
        ):
            xf_copies.append(pltpu.make_async_copy(
                src, xf.at[pl.ds(at, src.shape[0])], xsem.at[len(xf_copies)]))

    def field_load(i):
        some = pl.ds(i * STEP, STEP)
        return pltpu.make_async_copy(field_in.at[:, some], field.at[:, some], fsem.at[i])

    @pl.loop(0, comps_half // STEP)
    def _(i):
        field_load(i).start()

    barrier = pltpu.get_barrier_semaphore()
    for s in range(1, gx):
        pl.semaphore_signal(
            barrier, inc=1, device_id={"gx": lax.rem(me_x + s, gx)}, device_id_type=MESH)
    for s in range(1, gy):
        pl.semaphore_signal(
            barrier, inc=1, device_id={"gy": lax.rem(me_y + s, gy)}, device_id_type=MESH)
    pl.semaphore_wait(barrier, gx + gy - 2)

    def remote(src, dst, send, recv, axis, peer):
        return pltpu.make_async_remote_copy(
            src_ref=src, dst_ref=dst, send_sem=send, recv_sem=recv,
            device_id={axis: peer}, device_id_type=MESH)

    def lines_of(ref, j, g):
        return ref.at[:, :, pl.ds(pl.multiple_of((j * gx + g) * rows, rows), rows), :]

    def out_x(j):
        copies = []
        for s in range(1, gx):
            peer = lax.rem(me_x + s, gx)
            copies.append(remote(first.at[j % SLOTS, peer], xb.at[j, me_x],
                                 b_send.at[j, s - 1], b_recv.at[j, s - 1], "gx", peer))
        mine = pltpu.make_async_copy(first.at[j % SLOTS, me_x], xb.at[j, me_x], own.at[0, j])
        return copies, mine

    def out_y(j):
        copies = []
        for s in range(1, gy):
            peer = lax.rem(me_y + s, gy)
            copies.append(remote(
                sec.at[j % SLOTS, pl.ds(peer * CHUNK_ROWS, CHUNK_ROWS)],
                col.at[j, :, pl.ds(pl.multiple_of(me_y * comps, comps), comps), :],
                d_send.at[j, s - 1], d_recv.at[j, s - 1], "gy", peer))
        mine = pltpu.make_async_copy(
            sec.at[j % SLOTS, pl.ds(me_y * CHUNK_ROWS, CHUNK_ROWS)],
            col.at[j, :, pl.ds(pl.multiple_of(me_y * comps, comps), comps), :], own.at[1, j])
        return copies, mine

    def back_y(j):
        copies = []
        for s in range(1, gy):
            peer = lax.rem(me_y + s, gy)
            copies.append(remote(
                col.at[j, :, pl.ds(pl.multiple_of(peer * comps, comps), comps), :],
                ret.at[j, pl.ds(me_y * CHUNK_ROWS, CHUNK_ROWS)],
                e_send.at[j, s - 1], e_recv.at[j, s - 1], "gy", peer))
        mine = pltpu.make_async_copy(
            col.at[j, :, pl.ds(pl.multiple_of(me_y * comps, comps), comps), :],
            ret.at[j, pl.ds(me_y * CHUNK_ROWS, CHUNK_ROWS)], own.at[2, j])
        return copies, mine

    def back_x(j):
        copies = []
        for s in range(1, gx):
            peer = lax.rem(me_x + s, gx)
            copies.append(remote(xb.at[j, peer], lines_of(ylines, j, me_x),
                                 f_send.at[j, s - 1], f_recv.at[j, s - 1], "gx", peer))
        mine = pltpu.make_async_copy(xb.at[j, me_x], lines_of(ylines, j, me_x), own.at[3, j])
        return copies, mine

    def start(pair):
        for copy in pair[0]:
            copy.start()
        pair[1].start()
        return pair

    def arrive(pair):
        for copy in pair[0]:
            copy.wait_recv()
        pair[1].wait()

    def drain(pair):
        for copy in pair[0]:
            copy.wait_send()

    def norm_load(j):
        return pltpu.make_async_copy(norm.at[pl.ds(j * CHUNK_ROWS, CHUNK_ROWS)], nbuf, nsem)

    odd = lax.rem(me_x, 2)

    def first_lines(j):
        @pl.loop(0, comps_half // STEP)
        def _(i):
            if j == 0:
                field_load(i).wait()
            cs = [i * STEP + c for c in range(STEP)]
            parts = [field[h, c, :LANES, :] for h in range(2) for c in cs]
            for c in cs:
                parts += [field[odd, c, LANES:, :], field[1 - odd, c, LANES:, :]]
            result = lax.dot_general(
                yf[j * gx * rows:(j + 1) * gx * rows, :], jnp.concatenate(parts, 0),
                (((1,), (1,)), ((), ())), preferred_element_type=jnp.float32)
            for t in range(3):
                for c in range(STEP):
                    at = (t * STEP + c) * LANES
                    lines = result[:, at:at + LANES].astype(jnp.bfloat16)
                    for g in range(gx):
                        first[j % SLOTS, g, t, cs[c]] = lines[g * rows:(g + 1) * rows]

    def low_lanes(shape):
        return lax.broadcasted_iota(jnp.int32, shape, len(shape) - 1) < HALF

    def forward(j):
        for h in range(2):
            for g in range(gx):
                xs[:, g * LANES:(g + 1) * LANES] = xb[j, g, h].reshape(m, LANES)
            for q in range(gx // 2):
                even = xb[j, 2 * q, 2].reshape(m, LANES)
                odd = xb[j, 2 * q + 1, 2].reshape(m, LANES)
                low, high = (even, odd) if h == 0 else (odd, even)
                at = whole_a + q * LANES
                xs[:, at:at + LANES] = jnp.where(low_lanes((m, LANES)), low, high)
            base = whole_a + part_b * h

            @pl.loop(0, width // TILE)
            def _(n):
                cols = pl.ds(pl.multiple_of(n * TILE, TILE), TILE)
                acc = jnp.dot(xs[:, :whole_a], xf[:whole_a, cols],
                              preferred_element_type=jnp.float32)
                acc += jnp.dot(xs[:, whole_a:], xf[base:base + part_b, cols],
                               preferred_element_type=jnp.float32)
                for i in range(TILE // LANES):
                    spread[i] = acc[:, i * LANES:(i + 1) * LANES]
                for i in range(TILE // LANES):
                    lanes = pl.ds(pl.multiple_of(n * TILE + i * LANES, LANES), LANES)
                    for y in range(rows):
                        line = spread[i, pl.ds(y, comps_half, stride=rows), :]
                        sec[j % SLOTS, y, h * comps_half:(h + 1) * comps_half, lanes] = (
                            line.astype(jnp.bfloat16))

    def columns(j):
        @pl.loop(0, CHUNK_ROWS)
        def _(r):
            for s in range(species):
                here = slice(s * levels, (s + 1) * levels)
                for n in range(0, width, 2 * TILE):
                    lanes = slice(n, n + 2 * TILE)
                    scales = nbuf[r, here, lanes]
                    scaled = scales * col[j, r, here, lanes].astype(jnp.float32)
                    high = scaled.astype(jnp.bfloat16)
                    low = (scaled - high.astype(jnp.float32)).astype(jnp.bfloat16)
                    stack = jnp.concatenate([high, high, low], axis=0)
                    raised = jnp.dot(factor[s], stack, preferred_element_type=jnp.float32)
                    col[j, r, here, lanes] = (scales * raised).astype(jnp.bfloat16)

    def adjoint(j):
        def lines(h):
            return ret[j, :, h * comps_half:(h + 1) * comps_half, :].reshape(m, width)

        def put(part, g, t, i):
            spread[i] = part
            for c in range(comps_half):
                line = spread[i, pl.ds(c, rows, stride=comps_half), :]
                xb[j, g, t, c] = line.astype(jnp.bfloat16)

        def dots(block, at):
            return lax.dot_general(block, xf[pl.ds(at, TILE), :], (((1,), (1,)), ((), ())),
                                   preferred_element_type=jnp.float32)

        for h in range(2):
            @pl.loop(0, whole_a // TILE)
            def _(n):
                part = dots(lines(h), pl.multiple_of(n * TILE, TILE))
                for i in range(TILE // LANES):
                    put(part[:, i * LANES:(i + 1) * LANES], n * (TILE // LANES) + i, h, i)

        @pl.loop(0, part_b // TILE)
        def _(n):
            at = pl.multiple_of(whole_a + n * TILE, TILE)
            part0 = dots(lines(0), at)
            part1 = dots(lines(1), pl.multiple_of(at + part_b, TILE))
            for i in range(TILE // LANES):
                p0 = part0[:, i * LANES:(i + 1) * LANES]
                p1 = part1[:, i * LANES:(i + 1) * LANES]
                mask = low_lanes((m, LANES))
                g = 2 * (n * (TILE // LANES) + i)
                put(jnp.where(mask, p0, p1), g, 2, 0)
                put(jnp.where(mask, p1, p0), g + 1, 2, 1)

    bs, ds, es, fs = {}, {}, {}, {}

    def stage_c(j):
        arrive(bs[j])
        if j >= SLOTS:
            drain(ds[j - SLOTS])
        forward(j)
        ds[j] = start(out_y(j))
        if j + SLOTS < chunks:
            drain(bs[j])
            first_lines(j + SLOTS)
            bs[j + SLOTS] = start(out_x(j + SLOTS))

    def stage_e(j):
        arrive(ds[j])
        norm_load(j).wait()
        columns(j)
        es[j] = start(back_y(j))
        if j + 1 < chunks:
            norm_load(j + 1).start()

    def stage_f(j):
        arrive(es[j])
        adjoint(j)
        fs[j] = start(back_x(j))

    for j in range(min(SLOTS, chunks)):
        first_lines(j)
        bs[j] = start(out_x(j))
    for copy in xf_copies:
        copy.start()
    norm_load(0).start()
    for copy in xf_copies:
        copy.wait()
    stage_c(0)
    stage_e(0)
    for j in range(1, chunks):
        stage_c(j)
        stage_f(j - 1)
        stage_e(j)
    stage_f(chunks - 1)
    for j in range(chunks):
        arrive(fs[j])
    for j in range(chunks):
        for pair, slots in ((bs[j], SLOTS), (ds[j], SLOTS), (es[j], 0), (fs[j], 0)):
            if j + slots >= chunks or slots == 0:
                drain(pair)


def exchange(gx, gy, field, norm_field, x_filter, factor, yf):
    _, comps_half, strip, lines = field.shape
    rows = gy * CHUNK_ROWS
    chunks = lines // (gx * rows)
    width = x_filter.shape[1]
    dma = pltpu.SemaphoreType.DMA
    all_comps = norm_field.shape[1]
    return pl.pallas_call(
        functools.partial(exchange_kernel, gx, gy),
        out_shape=jax.ShapeDtypeStruct((3, comps_half, lines, LANES), jnp.bfloat16),
        in_specs=[
            pl.BlockSpec(memory_space=pl.ANY),
            pl.BlockSpec(memory_space=pl.ANY),
            pl.BlockSpec(memory_space=pl.ANY),
            pl.BlockSpec(memory_space=pltpu.VMEM),
            pl.BlockSpec(memory_space=pltpu.VMEM),
        ],
        out_specs=pl.BlockSpec(memory_space=pl.ANY),
        scratch_shapes=[
            pltpu.VMEM((chunks, gx, 3, comps_half, rows, LANES), jnp.bfloat16),
            pltpu.VMEM((SLOTS, rows, 2 * comps_half, width), jnp.bfloat16),
            pltpu.VMEM((chunks, CHUNK_ROWS, all_comps, width), jnp.bfloat16),
            pltpu.VMEM((chunks, rows, 2 * comps_half, width), jnp.bfloat16),
            pltpu.VMEM((rows * comps_half, width), jnp.bfloat16),
            pltpu.VMEM((CHUNK_ROWS, all_comps, width), jnp.float32),
            pltpu.VMEM((gx * (LANES + 2 * HALF), width), jnp.bfloat16),
            pltpu.VMEM((TILE // LANES, rows * comps_half, LANES), jnp.float32),
            pltpu.VMEM(field.shape, jnp.bfloat16),
            pltpu.VMEM((SLOTS, gx, 3, comps_half, rows, LANES), jnp.bfloat16),
            dma((chunks, gx - 1)), dma((chunks, gx - 1)),
            dma((chunks, gy - 1)), dma((chunks, gy - 1)),
            dma((chunks, gy - 1)), dma((chunks, gy - 1)),
            dma((chunks, gx - 1)), dma((chunks, gx - 1)),
            dma((4, chunks)), dma, dma((3 * gx,)), dma((comps_half // STEP,)),
        ],
        compiler_params=pltpu.CompilerParams(
            collective_id=0, has_side_effects=True, vmem_limit_bytes=60 * 1024 * 1024),
        name="exchange",
    )(field, norm_field, x_filter, factor, yf)


def last_kernel(yf, ylines, result):
    odd = lax.rem(lax.axis_index("gx"), 2)
    comps = ylines.shape[1]
    lines = jnp.concatenate(
        [ylines[t, c] for t in range(3) for c in range(comps)], 1)
    total = jnp.dot(lines.T, yf[...], preferred_element_type=jnp.float32).astype(jnp.bfloat16)
    for c in range(comps):
        for h in range(2):
            at = (h * comps + c) * LANES
            result[h, c, :LANES, :] = total[at:at + LANES]
        at = (2 * comps + c) * LANES
        result[odd, c, LANES:, :] = total[at:at + HALF]
        result[1 - odd, c, LANES:, :] = total[at + HALF:at + LANES]


def last_lines(yf, ylines):
    _, half, lines, _ = ylines.shape
    strip = LANES + HALF
    step = STEP
    return pl.pallas_call(
        last_kernel,
        grid=(half // step,),
        out_shape=jax.ShapeDtypeStruct((2, half, strip, lines), jnp.bfloat16),
        in_specs=[
            pl.BlockSpec((lines, lines), lambda i: (0, 0)),
            pl.BlockSpec((3, step, lines, LANES), lambda i: (0, i, 0, 0)),
        ],
        out_specs=pl.BlockSpec((2, step, strip, lines), lambda i: (0, i, 0, 0)),
        compiler_params=pltpu.CompilerParams(vmem_limit_bytes=48 * 1024 * 1024),
        name="last_lines",
    )(yf, ylines)


def fused_plan(gx, gy, field, norm_field, vertical, x_filter, y_filter):
    lines, comps, width = field.shape
    chunks = norm_field.shape[0] // CHUNK_ROWS
    half = comps // 2

    product = jnp.einsum("skl,sml->skm", vertical, vertical, precision=lax.Precision.HIGHEST)
    high = lax.reduce_precision(product, 8, 7)
    low = product - high
    factor = jnp.concatenate([high, low, high], 2).astype(jnp.bfloat16)

    yf = y_filter.reshape(lines, gx, gy, chunks, CHUNK_ROWS)
    yf = yf.transpose(3, 1, 2, 4, 0).reshape(lines, lines)

    strips = field.transpose(1, 2, 0).reshape(2, half, width, lines)
    ylines = exchange(gx, gy, strips, norm_field, x_filter, factor, yf)
    result = last_lines(yf, ylines)
    return result.reshape(comps, width, lines).transpose(2, 0, 1)


def per_device(gx, gy, field, norm_field, vertical, x_filter, y_filter):
    lines, comps, width = field.shape
    rows, all_comps, whole = norm_field.shape
    fits = (
        width == LANES + HALF and comps == 32 and rows % CHUNK_ROWS == 0 and gy * CHUNK_ROWS % 16 == 0 and gx % 4 == 0
        and gy > 1 and whole % (2 * TILE) == 0 and vertical.shape[1] % 16 == 0
        and rows * all_comps * whole <= 24 * 128 * 1536
    )
    if fits:
        return fused_plan(gx, gy, field, norm_field, vertical, x_filter, y_filter)
    return general_plan(field, norm_field, vertical, x_filter, y_filter)


def solution(mesh):
    return jax.shard_map(
        functools.partial(per_device, mesh.shape["gx"], mesh.shape["gy"]),
        mesh=mesh,
        in_specs=(P(None, "gy", "gx"), P(("gx", "gy"), None, None), P(), P(), P()),
        out_specs=P(None, "gy", "gx"),
        check_vma=False,
    )
```

```python
import functools

import jax
import jax.numpy as jnp
from jax import lax
from jax.experimental import pallas as pl
from jax.experimental.pallas import tpu as pltpu
from jax.sharding import PartitionSpec as P

MESH = pl.DeviceIdType.MESH
LANES = 128
HALF = 64
CHUNK_ROWS = 4
SLOTS = 3
STEP = 2
LAG = 3
TILE = 256


def xlines_forward(block, x_filter):
    width = x_filter.shape[0]
    result = jnp.dot(block.reshape(-1, width), x_filter, preferred_element_type=jnp.float32)
    return result.astype(jnp.bfloat16).reshape(block.shape)


def xlines_adjoint(block, x_filter):
    width = x_filter.shape[0]
    result = lax.dot_general(
        block.reshape(-1, width),
        x_filter,
        (((1,), (1,)), ((), ())),
        preferred_element_type=jnp.float32,
    )
    return result.astype(jnp.bfloat16).reshape(block.shape)


def columns_work(block, scales, vertical):
    species = vertical.shape[0]
    levels = vertical.shape[1]
    rows, comps, width = block.shape
    scaled = (scales * block.astype(jnp.float32)).reshape(rows, species, levels, width)
    lowered = jnp.einsum("slk,rslx->rskx", vertical, scaled, precision=lax.Precision.HIGHEST)
    raised = jnp.einsum("skl,rslx->rskx", vertical, lowered, precision=lax.Precision.HIGHEST)
    return (scales * raised.reshape(rows, comps, width)).astype(jnp.bfloat16)


def general_plan(field, norm_field, vertical, x_filter, y_filter):
    lines, comps, width = field.shape
    first = lax.dot_general(
        y_filter,
        field.reshape(lines, comps * width),
        (((0,), (0,)), ((), ())),
        preferred_element_type=jnp.float32,
    )
    first = first.astype(jnp.bfloat16).reshape(lines, comps, width)
    xblock = lax.all_to_all(first, "gx", split_axis=0, concat_axis=2, tiled=True)
    second = xlines_forward(xblock, x_filter)
    columns = lax.all_to_all(second, "gy", split_axis=0, concat_axis=1, tiled=True)
    middle = columns_work(columns, norm_field, vertical)
    returned = lax.all_to_all(middle, "gy", split_axis=1, concat_axis=0, tiled=True)
    third = xlines_adjoint(returned, x_filter)
    ylines = lax.all_to_all(third, "gx", split_axis=2, concat_axis=0, tiled=True)
    result = jnp.dot(
        y_filter, ylines.reshape(lines, comps * width), preferred_element_type=jnp.float32
    )
    return result.astype(jnp.bfloat16).reshape(lines, comps, width)


def exchange_kernel(
    gx, gy, field_in, norm, x_filter, factor, yf, ylines,
    xb, sec, col, ret, xs, nbuf, xf, spread, field, first,
    b_send, b_recv, d_send, d_recv, e_send, e_recv, f_send, f_recv, own, nsem, xsem, fsem,
):
    chunks, _, _, comps_half, rows, _ = xb.shape
    comps = 2 * comps_half
    width = xf.shape[1]
    species, levels, _ = factor.shape
    me_x = lax.axis_index("gx")
    me_y = lax.axis_index("gy")
    whole_a = gx * LANES
    part_b = gx * HALF
    m = rows * comps_half

    strip = LANES + HALF
    xf_copies = []
    for g in range(gx):
        tail = x_filter.at[pl.ds(g * strip + LANES, HALF)]
        for src, at in (
            (x_filter.at[pl.ds(g * strip, LANES)], g * LANES),
            (tail, whole_a + g * HALF),
            (tail, whole_a + part_b + (g ^ 1) * HALF),
        ):
            xf_copies.append(pltpu.make_async_copy(
                src, xf.at[pl.ds(at, src.shape[0])], xsem.at[len(xf_copies)]))

    def field_load(i):
        some = pl.ds(i * STEP, STEP)
        return pltpu.make_async_copy(field_in.at[:, some], field.at[:, some], fsem.at[i])

    @pl.loop(0, comps_half // STEP)
    def _(i):
        field_load(i).start()

    barrier = pltpu.get_barrier_semaphore()
    for s in range(1, gx):
        pl.semaphore_signal(
            barrier, inc=1, device_id={"gx": lax.rem(me_x + s, gx)}, device_id_type=MESH)
    for s in range(1, gy):
        pl.semaphore_signal(
            barrier, inc=1, device_id={"gy": lax.rem(me_y + s, gy)}, device_id_type=MESH)
    pl.semaphore_wait(barrier, gx + gy - 2)

    def remote(src, dst, send, recv, axis, peer):
        return pltpu.make_async_remote_copy(
            src_ref=src, dst_ref=dst, send_sem=send, recv_sem=recv,
            device_id={axis: peer}, device_id_type=MESH)

    def lines_of(ref, j, g):
        return ref.at[:, :, pl.ds(pl.multiple_of((j * gx + g) * rows, rows), rows), :]

    def out_x(j):
        copies = []
        for s in range(1, gx):
            peer = lax.rem(me_x + s, gx)
            copies.append(remote(first.at[j % SLOTS, peer], xb.at[j, me_x],
                                 b_send.at[j, s - 1], b_recv.at[j, s - 1], "gx", peer))
        mine = pltpu.make_async_copy(first.at[j % SLOTS, me_x], xb.at[j, me_x], own.at[0, j])
        return copies, mine

    def out_y(j):
        copies = []
        for s in range(1, gy):
            peer = lax.rem(me_y + s, gy)
            copies.append(remote(
                sec.at[j % SLOTS, pl.ds(peer * CHUNK_ROWS, CHUNK_ROWS)],
                col.at[j, :, pl.ds(pl.multiple_of(me_y * comps, comps), comps), :],
                d_send.at[j, s - 1], d_recv.at[j, s - 1], "gy", peer))
        mine = pltpu.make_async_copy(
            sec.at[j % SLOTS, pl.ds(me_y * CHUNK_ROWS, CHUNK_ROWS)],
            col.at[j, :, pl.ds(pl.multiple_of(me_y * comps, comps), comps), :], own.at[1, j])
        return copies, mine

    def back_y(j):
        copies = []
        for s in range(1, gy):
            peer = lax.rem(me_y + s, gy)
            copies.append(remote(
                col.at[j, :, pl.ds(pl.multiple_of(peer * comps, comps), comps), :],
                ret.at[j, pl.ds(me_y * CHUNK_ROWS, CHUNK_ROWS)],
                e_send.at[j, s - 1], e_recv.at[j, s - 1], "gy", peer))
        mine = pltpu.make_async_copy(
            col.at[j, :, pl.ds(pl.multiple_of(me_y * comps, comps), comps), :],
            ret.at[j, pl.ds(me_y * CHUNK_ROWS, CHUNK_ROWS)], own.at[2, j])
        return copies, mine

    def back_x(j):
        copies = []
        for s in range(1, gx):
            peer = lax.rem(me_x + s, gx)
            copies.append(remote(xb.at[j, peer], lines_of(ylines, j, me_x),
                                 f_send.at[j, s - 1], f_recv.at[j, s - 1], "gx", peer))
        mine = pltpu.make_async_copy(xb.at[j, me_x], lines_of(ylines, j, me_x), own.at[3, j])
        return copies, mine

    def start(pair):
        for copy in pair[0]:
            copy.start()
        pair[1].start()
        return pair

    def arrive(pair):
        for copy in pair[0]:
            copy.wait_recv()
        pair[1].wait()

    def drain(pair):
        for copy in pair[0]:
            copy.wait_send()

    def norm_load(j):
        return pltpu.make_async_copy(norm.at[pl.ds(j * CHUNK_ROWS, CHUNK_ROWS)], nbuf, nsem)

    odd = lax.rem(me_x, 2)

    def first_lines(j):
        @pl.loop(0, comps_half // STEP)
        def _(i):
            if j == 0:
                field_load(i).wait()
            cs = [i * STEP + c for c in range(STEP)]
            parts = [field[h, c, :LANES, :] for h in range(2) for c in cs]
            for c in cs:
                parts += [field[odd, c, LANES:, :], field[1 - odd, c, LANES:, :]]
            result = lax.dot_general(
                yf[j * gx * rows:(j + 1) * gx * rows, :], jnp.concatenate(parts, 0),
                (((1,), (1,)), ((), ())), preferred_element_type=jnp.float32)
            for t in range(3):
                for c in range(STEP):
                    at = (t * STEP + c) * LANES
                    lines = result[:, at:at + LANES].astype(jnp.bfloat16)
                    for g in range(gx):
                        first[j % SLOTS, g, t, cs[c]] = lines[g * rows:(g + 1) * rows]

    def low_lanes(shape):
        return lax.broadcasted_iota(jnp.int32, shape, len(shape) - 1) < HALF

    def forward(j):
        for h in range(2):
            for g in range(gx):
                xs[:, g * LANES:(g + 1) * LANES] = xb[j, g, h].reshape(m, LANES)
            for q in range(gx // 2):
                even = xb[j, 2 * q, 2].reshape(m, LANES)
                odd = xb[j, 2 * q + 1, 2].reshape(m, LANES)
                low, high = (even, odd) if h == 0 else (odd, even)
                at = whole_a + q * LANES
                xs[:, at:at + LANES] = jnp.where(low_lanes((m, LANES)), low, high)
            base = whole_a + part_b * h

            @pl.loop(0, width // TILE)
            def _(n):
                cols = pl.ds(pl.multiple_of(n * TILE, TILE), TILE)
                acc = jnp.dot(xs[:, :whole_a], xf[:whole_a, cols],
                              preferred_element_type=jnp.float32)
                acc += jnp.dot(xs[:, whole_a:], xf[base:base + part_b, cols],
                               preferred_element_type=jnp.float32)
                for i in range(TILE // LANES):
                    spread[i] = acc[:, i * LANES:(i + 1) * LANES]
                for i in range(TILE // LANES):
                    lanes = pl.ds(pl.multiple_of(n * TILE + i * LANES, LANES), LANES)
                    for y in range(rows):
                        line = spread[i, pl.ds(y, comps_half, stride=rows), :]
                        sec[j % SLOTS, y, h * comps_half:(h + 1) * comps_half, lanes] = (
                            line.astype(jnp.bfloat16))

    def columns(j):
        @pl.loop(0, CHUNK_ROWS)
        def _(r):
            for s in range(species):
                here = slice(s * levels, (s + 1) * levels)
                for n in range(0, width, 2 * TILE):
                    lanes = slice(n, n + 2 * TILE)
                    scales = nbuf[r, here, lanes]
                    scaled = scales * col[j, r, here, lanes].astype(jnp.float32)
                    high = scaled.astype(jnp.bfloat16)
                    low = (scaled - high.astype(jnp.float32)).astype(jnp.bfloat16)
                    stack = jnp.concatenate([high, high, low], axis=0)
                    raised = jnp.dot(factor[s], stack, preferred_element_type=jnp.float32)
                    col[j, r, here, lanes] = (scales * raised).astype(jnp.bfloat16)

    def adjoint(j):
        def lines(h):
            return ret[j, :, h * comps_half:(h + 1) * comps_half, :].reshape(m, width)

        def put(part, g, t, i):
            spread[i] = part
            for c in range(comps_half):
                line = spread[i, pl.ds(c, rows, stride=comps_half), :]
                xb[j, g, t, c] = line.astype(jnp.bfloat16)

        def dots(block, at):
            return lax.dot_general(block, xf[pl.ds(at, TILE), :], (((1,), (1,)), ((), ())),
                                   preferred_element_type=jnp.float32)

        for h in range(2):
            @pl.loop(0, whole_a // TILE)
            def _(n):
                part = dots(lines(h), pl.multiple_of(n * TILE, TILE))
                for i in range(TILE // LANES):
                    put(part[:, i * LANES:(i + 1) * LANES], n * (TILE // LANES) + i, h, i)

        @pl.loop(0, part_b // TILE)
        def _(n):
            at = pl.multiple_of(whole_a + n * TILE, TILE)
            part0 = dots(lines(0), at)
            part1 = dots(lines(1), pl.multiple_of(at + part_b, TILE))
            for i in range(TILE // LANES):
                p0 = part0[:, i * LANES:(i + 1) * LANES]
                p1 = part1[:, i * LANES:(i + 1) * LANES]
                mask = low_lanes((m, LANES))
                g = 2 * (n * (TILE // LANES) + i)
                put(jnp.where(mask, p0, p1), g, 2, 0)
                put(jnp.where(mask, p1, p0), g + 1, 2, 1)

    bs, ds, es, fs = {}, {}, {}, {}

    def stage_c(j):
        arrive(bs[j])
        if j >= SLOTS:
            drain(ds[j - SLOTS])
        forward(j)
        ds[j] = start(out_y(j))
        if j + SLOTS < chunks:
            drain(bs[j])
            first_lines(j + SLOTS)
            bs[j + SLOTS] = start(out_x(j + SLOTS))

    def stage_e(j):
        arrive(ds[j])
        norm_load(j).wait()
        columns(j)
        es[j] = start(back_y(j))
        if j + 1 < chunks:
            norm_load(j + 1).start()

    def stage_f(j):
        arrive(es[j])
        adjoint(j)
        fs[j] = start(back_x(j))

    for j in range(min(SLOTS, chunks)):
        first_lines(j)
        bs[j] = start(out_x(j))
    for copy in xf_copies:
        copy.start()
    norm_load(0).start()
    for copy in xf_copies:
        copy.wait()
    for j in range(chunks + LAG):
        if j < chunks:
            stage_c(j)
        if 1 <= j <= chunks:
            stage_e(j - 1)
        if j >= LAG:
            stage_f(j - LAG)
    for j in range(chunks):
        arrive(fs[j])
    for j in range(chunks):
        for pair, slots in ((bs[j], SLOTS), (ds[j], SLOTS), (es[j], 0), (fs[j], 0)):
            if j + slots >= chunks or slots == 0:
                drain(pair)


def exchange(gx, gy, field, norm_field, x_filter, factor, yf):
    _, comps_half, strip, lines = field.shape
    rows = gy * CHUNK_ROWS
    chunks = lines // (gx * rows)
    width = x_filter.shape[1]
    dma = pltpu.SemaphoreType.DMA
    all_comps = norm_field.shape[1]
    return pl.pallas_call(
        functools.partial(exchange_kernel, gx, gy),
        out_shape=jax.ShapeDtypeStruct((3, comps_half, lines, LANES), jnp.bfloat16),
        in_specs=[
            pl.BlockSpec(memory_space=pl.ANY),
            pl.BlockSpec(memory_space=pl.ANY),
            pl.BlockSpec(memory_space=pl.ANY),
            pl.BlockSpec(memory_space=pltpu.VMEM),
            pl.BlockSpec(memory_space=pltpu.VMEM),
        ],
        out_specs=pl.BlockSpec(memory_space=pl.ANY),
        scratch_shapes=[
            pltpu.VMEM((chunks, gx, 3, comps_half, rows, LANES), jnp.bfloat16),
            pltpu.VMEM((SLOTS, rows, 2 * comps_half, width), jnp.bfloat16),
            pltpu.VMEM((chunks, CHUNK_ROWS, all_comps, width), jnp.bfloat16),
            pltpu.VMEM((chunks, rows, 2 * comps_half, width), jnp.bfloat16),
            pltpu.VMEM((rows * comps_half, width), jnp.bfloat16),
            pltpu.VMEM((CHUNK_ROWS, all_comps, width), jnp.float32),
            pltpu.VMEM((gx * (LANES + 2 * HALF), width), jnp.bfloat16),
            pltpu.VMEM((TILE // LANES, rows * comps_half, LANES), jnp.float32),
            pltpu.VMEM(field.shape, jnp.bfloat16),
            pltpu.VMEM((SLOTS, gx, 3, comps_half, rows, LANES), jnp.bfloat16),
            dma((chunks, gx - 1)), dma((chunks, gx - 1)),
            dma((chunks, gy - 1)), dma((chunks, gy - 1)),
            dma((chunks, gy - 1)), dma((chunks, gy - 1)),
            dma((chunks, gx - 1)), dma((chunks, gx - 1)),
            dma((4, chunks)), dma, dma((3 * gx,)), dma((comps_half // STEP,)),
        ],
        compiler_params=pltpu.CompilerParams(
            collective_id=0, has_side_effects=True, vmem_limit_bytes=60 * 1024 * 1024),
        name="exchange",
    )(field, norm_field, x_filter, factor, yf)


def last_kernel(yf, ylines, result):
    odd = lax.rem(lax.axis_index("gx"), 2)
    comps = ylines.shape[1]
    lines = jnp.concatenate(
        [ylines[t, c] for t in range(3) for c in range(comps)], 1)
    total = jnp.dot(lines.T, yf[...], preferred_element_type=jnp.float32).astype(jnp.bfloat16)
    for c in range(comps):
        for h in range(2):
            at = (h * comps + c) * LANES
            result[h, c, :LANES, :] = total[at:at + LANES]
        at = (2 * comps + c) * LANES
        result[odd, c, LANES:, :] = total[at:at + HALF]
        result[1 - odd, c, LANES:, :] = total[at + HALF:at + LANES]


def last_lines(yf, ylines):
    _, half, lines, _ = ylines.shape
    strip = LANES + HALF
    step = STEP
    return pl.pallas_call(
        last_kernel,
        grid=(half // step,),
        out_shape=jax.ShapeDtypeStruct((2, half, strip, lines), jnp.bfloat16),
        in_specs=[
            pl.BlockSpec((lines, lines), lambda i: (0, 0)),
            pl.BlockSpec((3, step, lines, LANES), lambda i: (0, i, 0, 0)),
        ],
        out_specs=pl.BlockSpec((2, step, strip, lines), lambda i: (0, i, 0, 0)),
        compiler_params=pltpu.CompilerParams(vmem_limit_bytes=48 * 1024 * 1024),
        name="last_lines",
    )(yf, ylines)


def fused_plan(gx, gy, field, norm_field, vertical, x_filter, y_filter):
    lines, comps, width = field.shape
    chunks = norm_field.shape[0] // CHUNK_ROWS
    half = comps // 2

    product = jnp.einsum("skl,sml->skm", vertical, vertical, precision=lax.Precision.HIGHEST)
    high = lax.reduce_precision(product, 8, 7)
    low = product - high
    factor = jnp.concatenate([high, low, high], 2).astype(jnp.bfloat16)

    yf = y_filter.reshape(lines, gx, gy, chunks, CHUNK_ROWS)
    yf = yf.transpose(3, 1, 2, 4, 0).reshape(lines, lines)

    strips = field.transpose(1, 2, 0).reshape(2, half, width, lines)
    ylines = exchange(gx, gy, strips, norm_field, x_filter, factor, yf)
    result = last_lines(yf, ylines)
    return result.reshape(comps, width, lines).transpose(2, 0, 1)


def per_device(gx, gy, field, norm_field, vertical, x_filter, y_filter):
    lines, comps, width = field.shape
    rows, all_comps, whole = norm_field.shape
    fits = (
        width == LANES + HALF and comps == 32 and rows % CHUNK_ROWS == 0 and gy * CHUNK_ROWS % 16 == 0 and gx % 4 == 0
        and gy > 1 and whole % (2 * TILE) == 0 and vertical.shape[1] % 16 == 0
        and rows * all_comps * whole <= 24 * 128 * 1536
    )
    if fits:
        return fused_plan(gx, gy, field, norm_field, vertical, x_filter, y_filter)
    return general_plan(field, norm_field, vertical, x_filter, y_filter)


def solution(mesh):
    return jax.shard_map(
        functools.partial(per_device, mesh.shape["gx"], mesh.shape["gy"]),
        mesh=mesh,
        in_specs=(P(None, "gy", "gx"), P(("gx", "gy"), None, None), P(), P(), P()),
        out_specs=P(None, "gy", "gx"),
        check_vma=False,
    )
```
